32 devices in a mesh: seq: 16 (over z, x, core), cand: 2 (over y).
Axes of the slice: x: 2, y: 2, z: 4, core: 2. Of those that a mesh axis runs over, the one named last changes fastest.
Arguments:
- behaviors: float32 [2, 131072, 128], P('cand', 'seq'), may hold values from -15 to 15
- cluster_ids: int32 [2, 131072], P('cand', 'seq'), may hold values from 0 to 2047, as said below
- lengths: int32 [2, 16], P('cand', 'seq'), may hold values from 2048 to 8192
- candidates: bfloat16 [2, 1024, 128], P(None, ('seq', 'cand')), may hold values from -6 to 6
- w_query: bfloat16 [128, 128], replicated, may hold values from -0.5 to 0.5
- w_key: bfloat16 [128, 128], replicated, may hold values from -0.5 to 0.5
- w_hidden: bfloat16 [256, 512], replicated, may hold values from -0.375 to 0.375
- b_hidden: float32 [512], replicated, may hold values from -0.5 to 0.5
- w_out: float32 [512], replicated, may hold values from -0.25 to 0.25
Outputs:
- ranking: float32 [2, 1024], P(None, ('seq', 'cand'))
The draws below stay inside these ranges and needn't reach their ends.
Inputs may be any that keep to these rules, and one draw needn't show every extreme that they name: `cluster_ids`: each user's first 2048 slots name 2048 different clusters.
All inputs are finite; a program needn't handle non-finite values.
Results may differ from the reference program's by a relative error of at most 0.02.
Values may be sent and summed in bfloat16 or wider, within the bound.
No kernel may reach another device: no remote copies, remote signals or barrier semaphores. Data moves between devices by JAX's collectives and lax.ppermute only.
A program may use at most 64 MiB of HBM per device.

```python
import jax
import jax.numpy as jnp
from jax import lax

D = 128
C = 2048
H = 512
BEH_DEV = 8192
USERS = 2
HIST = 131072
NC = 1024
N_SEQ = 16


def shared_ids(key):
    base = jax.random.fold_in(key, 7301)
    first_key, second_key, third_key = jax.random.split(base, 3)
    bounds = jax.random.randint(first_key, (USERS, HIST), 1, C + 1)
    ranks = jax.random.randint(second_key, (USERS, HIST), 0, bounds)
    slot = jnp.arange(HIST, dtype=jnp.int32)
    ranks = jnp.where(slot[None, :] < C, slot[None, :], ranks).astype(jnp.int32)
    orders = jax.vmap(lambda k: jax.random.permutation(k, C))(jax.random.split(third_key, USERS)).astype(jnp.int32)
    return jax.vmap(lambda order, rank: order[rank])(orders, ranks).astype(jnp.int32)


def draw_cluster_ids(key, part):
    return shared_ids(key)


def draw_behaviors(key, part):
    ids = shared_ids(key)
    shards = HIST // BEH_DEV
    base = jax.random.fold_in(key, 9157)
    mean_key, drift_key, noise_key = jax.random.split(base, 3)
    means = jnp.clip(2.5 * jax.random.normal(mean_key, (USERS, C, D), jnp.float32), -6.0, 6.0)
    drift = jnp.clip(2.0 * jax.random.normal(drift_key, (USERS, shards * C, D), jnp.float32), -5.0, 5.0)
    noise = jnp.clip(jax.random.normal(noise_key, (USERS, HIST, D), jnp.float32), -4.0, 4.0)
    shard_of = (jnp.arange(HIST, dtype=jnp.int32) // BEH_DEV).astype(jnp.int32)
    drift_index = (shard_of[None, :] * C + ids).astype(jnp.int32)
    picked_means = jax.vmap(lambda table, index: table[index])(means, ids)
    picked_drift = jax.vmap(lambda table, index: table[index])(drift, drift_index)
    return jnp.clip(picked_means + picked_drift + noise, -15.0, 15.0)


def place_ends(result, own_key, smallest, largest):
    shape = result.shape
    place = [jax.random.randint(jax.random.fold_in(own_key, axis), (), 0, shape[axis]) for axis in range(len(shape))]
    result = result.at[tuple(place)].set(smallest)
    longest = shape.index(max(shape))
    place[longest] = (place[longest] + 1) % shape[longest]
    return result.at[tuple(place)].set(largest)


def steps_of(own_key, shape, cuts, least, high):
    def one(dim, parts):
        heights = jax.random.uniform(jax.random.fold_in(jax.random.fold_in(own_key, 6), dim), (parts,), jnp.float32, least / len(cuts), high / len(cuts))
        return jnp.repeat(jnp.exp(heights), shape[dim] // parts).reshape((-1,) + (1,) * (len(shape) - dim - 1))

    factor_of = one(*cuts[0])
    for cut in cuts[1:]:
        factor_of = factor_of * one(*cut)
    return factor_of


def scatter_about(own_key, dims, scale, bound, cuts=(), kind=jnp.bfloat16):
    drawn = scale * jax.random.normal(own_key, dims, jnp.float32)
    if cuts:
        drawn = drawn * steps_of(own_key, dims, cuts, -0.22, 0.18)
    return jnp.clip(drawn, -bound, bound).astype(kind)


def setup_inputs(seed: int = 0) -> dict:
    seeds = jax.random.split(jax.random.key(seed), 10)
    return {
        "behaviors": draw_behaviors(jax.random.fold_in(seeds[9], 71), 0),
        "cluster_ids": draw_cluster_ids(jax.random.fold_in(seeds[9], 71), 0),
        "lengths": place_ends(jax.random.randint(seeds[2], (USERS, N_SEQ), BEH_DEV // 4, BEH_DEV + 1), jax.random.fold_in(seeds[2], 1), BEH_DEV // 4, BEH_DEV).astype(jnp.int32),
        "candidates": scatter_about(seeds[3], (USERS, NC, D), 1.0, 6.0, ((1, 32),)),
        "w_query": scatter_about(seeds[4], (D, D), D ** -0.5, 0.5),
        "w_key": scatter_about(seeds[5], (D, D), D ** -0.5, 0.5),
        "w_hidden": scatter_about(seeds[6], (2 * D, H), (2 * D) ** -0.5, 0.375),
        "b_hidden": jnp.clip(jax.random.uniform(seeds[7], (H,), jnp.float32, -0.5, 0.5), -0.5, 0.5),
        "w_out": scatter_about(seeds[8], (H,), H ** -0.5, 0.25, (), jnp.float32),
    }


def one_user(item_rows, cluster_ids, length_row, cand_rows, w_query, w_key, w_hidden, b_hidden, w_out):
    within = jnp.arange(HIST, dtype=jnp.int32) % BEH_DEV
    limits = jnp.repeat(length_row, BEH_DEV)
    inside = within < limits
    masked = jnp.where(inside[:, None], item_rows, jnp.float32(0.0))
    sums = jax.ops.segment_sum(masked, cluster_ids, num_segments=C)
    counts = jax.ops.segment_sum(inside.astype(jnp.float32), cluster_ids, num_segments=C)
    centroids = (sums / jnp.maximum(counts, 1.0)[:, None]).astype(jnp.bfloat16)
    key_rows = jnp.dot(centroids, w_key, preferred_element_type=jnp.float32).astype(jnp.bfloat16)
    size_bias = jnp.where(counts > 0, jnp.log(1.0 + counts), jnp.float32(-1000000000.0)).astype(jnp.bfloat16)
    queries = jnp.dot(cand_rows, w_query, preferred_element_type=jnp.float32).astype(jnp.bfloat16)
    scores = jnp.dot(queries, key_rows.T, preferred_element_type=jnp.float32) / jnp.sqrt(jnp.float32(D))
    scores = scores + size_bias.astype(jnp.float32)[None, :]
    weights = jax.nn.softmax(scores, axis=-1).astype(jnp.bfloat16)
    attended = jnp.dot(weights, centroids, preferred_element_type=jnp.float32).astype(jnp.bfloat16)
    features = jnp.concatenate([cand_rows, attended], axis=-1)
    hidden = jax.nn.relu(jnp.dot(features, w_hidden, preferred_element_type=jnp.float32) + b_hidden)
    return jnp.dot(hidden, w_out, precision=lax.Precision.HIGHEST)

def reference(behaviors, cluster_ids, lengths, candidates, w_query, w_key, w_hidden, b_hidden, w_out):

    def single(packed):
        item_rows, ids, length_row, cand_rows = packed
        return one_user(item_rows, ids, length_row, cand_rows, w_query, w_key, w_hidden, b_hidden, w_out)
    return lax.map(single, (behaviors, cluster_ids, lengths, candidates))
```

```python
import functools

import jax
import jax.numpy as jnp
from jax import lax
from jax.experimental import pallas as pl
from jax.experimental.pallas import tpu as pltpu
from jax.sharding import PartitionSpec as P

CLUSTERS = 2048
BF = jnp.bfloat16
F32 = jnp.float32
PAD = 16
SHARERS = 4
NT = (((1,), (1,)), ((), ()))
TN = (((0,), (0,)), ((), ()))
NN = (((1,), (0,)), ((), ()))


def digit_plan(parts, slots):
    bits = 1
    while parts * (2 ** (bits + 1) - 1) <= 256:
        bits += 1
    return bits, -(-(slots.bit_length()) // bits)


def pool_kernel(
    width, low, bits, digits, scalars, ids_ref, rows_ref, send_ref, next_ref, mine_ref, total
):
    step, steps = pl.program_id(0), pl.num_programs(0)
    block = rows_ref.shape[0]
    groups = total.shape[0] // width
    turned = jnp.transpose(rows_ref[...]).astype(BF)
    ids = ids_ref[...]
    slot = step * block + lax.broadcasted_iota(jnp.int32, ids.shape, 1)
    shift = low.bit_length() - 1
    high = jnp.where(slot < scalars[0], (ids >> shift) ^ scalars[1], -1)
    high = high.astype(F32).astype(BF)
    within = (ids & (low - 1)).astype(F32).astype(BF)
    labels = lax.broadcasted_iota(jnp.int32, (low, 1), 0).astype(F32).astype(BF)
    onehot = jnp.where(labels == within, BF(1), BF(0))
    pieces = [jnp.where(high == BF(h), turned, BF(0)) for h in range(groups)]
    names = lax.broadcasted_iota(jnp.int32, (PAD, 1), 0).astype(F32).astype(BF)
    pieces.append(jnp.where(names == high, BF(1), BF(0)))
    part = lax.dot_general(
        jnp.concatenate(pieces, 0), onehot, NT, preferred_element_type=F32
    )

    @pl.when(step == 0)
    def _():
        total[...] = part

    @pl.when(step > 0)
    def _():
        total[...] += part

    @pl.when(step == steps - 1)
    def _():
        pairs = groups // 2
        counts = total[groups * width : groups * width + PAD, :].astype(jnp.int32)
        row = lax.broadcasted_iota(jnp.int32, (PAD, 1), 0)

        def block_of(pair):
            tally = jnp.zeros((PAD, low), jnp.int32)
            for k in range(2):
                for d in range(digits):
                    one = (counts[2 * pair + k : 2 * pair + k + 1, :] >> (bits * d)) & (2**bits - 1)
                    tally = jnp.where(row == k * digits + d, one, tally)
            return total[2 * pair * width : 2 * (pair + 1) * width, :], tally.astype(F32)

        for pair in range(pairs):
            sums, tally = block_of(pair)
            if pair == 0:
                dest = mine_ref
            elif pair == 1:
                dest = next_ref
            else:
                dest = send_ref.at[pair - 2]
            dest[: 2 * width, :] = sums.astype(dest.dtype)
            dest[2 * width :, :] = tally.astype(dest.dtype)


def pool(rows, ids, scalars, parts):
    slots, width = rows.shape
    low = CLUSTERS // (2 * SHARERS)
    bits, digits = digit_plan(parts, slots)
    block = min(2048, slots)
    groups = CLUSTERS // low
    height = 2 * width + PAD
    return pl.pallas_call(
        functools.partial(pool_kernel, width, low, bits, digits),
        grid=(slots // block,),
        in_specs=[
            pl.BlockSpec(memory_space=pltpu.SMEM),
            pl.BlockSpec((1, block), lambda b: (0, b)),
            pl.BlockSpec((block, width), lambda b: (b, 0)),
        ],
        out_specs=[
            pl.BlockSpec((2, height, low), lambda b: (0, 0, 0)),
            pl.BlockSpec((height, low), lambda b: (0, 0)),
            pl.BlockSpec((height, low), lambda b: (0, 0)),
        ],
        out_shape=[
            jax.ShapeDtypeStruct((2, height, low), BF),
            jax.ShapeDtypeStruct((height, low), F32),
            jax.ShapeDtypeStruct((height, low), F32),
        ],
        scratch_shapes=[pltpu.VMEM((groups * width + PAD, low), F32)],
        compiler_params=pltpu.CompilerParams(vmem_limit_bytes=40 << 20),
        name="pool",
    )(scalars, ids, rows)


def attend_kernel(width, bits, digits, own_ref, got_ref, cand_ref, wq_ref, wk_ref, out_ref):
    queries = jnp.dot(cand_ref[...], wq_ref[...], preferred_element_type=F32).astype(BF)
    total = own_ref[...].astype(F32) + got_ref[...].astype(F32)
    centroids, keys, biases = [], [], []
    for k in range(2):
        count = jnp.zeros((1, total.shape[1]), F32)
        for d in range(digits):
            row = 2 * width + k * digits + d
            count = count + total[row : row + 1, :] * F32(2 ** (bits * d))
        here = (total[k * width : (k + 1) * width, :] / jnp.maximum(count, 1.0)).astype(BF)
        centroids.append(here)
        keys.append(
            lax.dot_general(wk_ref[...], here, TN, preferred_element_type=F32).astype(BF)
        )
        bias = jnp.where(count > 0, jnp.log(1.0 + count), F32(-1e9))
        biases.append(bias.astype(BF).astype(F32))
    centroids = jnp.concatenate(centroids, 1)
    keys = jnp.concatenate(keys, 1)
    biases = jnp.concatenate(biases, 1)
    scores = jnp.dot(queries, keys, preferred_element_type=F32) * F32(width**-0.5) + biases
    peak = jnp.max(scores, axis=1, keepdims=True)
    weights = jnp.exp(scores - peak)
    mass = jnp.sum(weights, axis=1, keepdims=True)
    attended = lax.dot_general(weights.astype(BF), centroids, NT, preferred_element_type=F32)
    level = peak + jnp.log(mass)
    first = level.astype(BF).astype(F32)
    second = (level - first).astype(BF).astype(F32)
    third = level - first - second
    lane = lax.broadcasted_iota(jnp.int32, attended.shape, 1)
    levels = jnp.where(lane == 0, first, jnp.where(lane == 1, second, jnp.where(lane == 2, third, 0.0)))
    out_ref[:, :width] = (attended / mass).astype(BF)
    out_ref[:, width:] = levels.astype(BF)


def attend(own, got, cands, w_query, w_key, bits, digits):
    width = w_key.shape[0]
    return pl.pallas_call(
        functools.partial(attend_kernel, width, bits, digits),
        out_shape=jax.ShapeDtypeStruct((cands.shape[0], 2 * width), BF),
        compiler_params=pltpu.CompilerParams(vmem_limit_bytes=24 << 20),
        name="attend",
    )(own, got, cands, w_query, w_key)


def rank_kernel(users, got_ref, cand_ref, wh_ref, bh_ref, wo_ref, out_ref):
    width = cand_ref.shape[2]
    local = cand_ref.shape[1]
    joined = []
    for user in range(users):
        parts, levels = [], []
        for r in range(SHARERS):
            one = got_ref[r * users + user].astype(F32)
            parts.append(one[:, :width])
            levels.append(jnp.sum(one[:, width:], axis=1, keepdims=True))
        peak = functools.reduce(jnp.maximum, levels)
        shares = [jnp.exp(level - peak) for level in levels]
        mass = functools.reduce(jnp.add, shares)
        top = functools.reduce(jnp.add, [s * p for s, p in zip(shares, parts)])
        joined.append((top / mass).astype(BF))
    attended = jnp.concatenate(joined, 0)
    cands = cand_ref[...].reshape(users * local, width)
    hidden = jnp.dot(cands, wh_ref[:width, :], preferred_element_type=F32)
    hidden = hidden + jnp.dot(attended, wh_ref[width:, :], preferred_element_type=F32)
    hidden = jnp.maximum(hidden + bh_ref[...], 0.0) * wo_ref[...]
    lanes = 128
    folded = functools.reduce(
        jnp.add, [hidden[:, k : k + lanes] for k in range(0, hidden.shape[1], lanes)]
    )
    ranking = jnp.sum(jnp.transpose(folded), axis=0, keepdims=True)
    for user in range(users):
        out_ref[user : user + 1, :] = ranking[:, user * local : (user + 1) * local]


def rank(got, cands, w_hidden, b_hidden, w_out):
    users, local, width = cands.shape
    return pl.pallas_call(
        functools.partial(rank_kernel, users),
        out_shape=jax.ShapeDtypeStruct((users, local), F32),
        compiler_params=pltpu.CompilerParams(vmem_limit_bytes=16 << 20),
        name="rank",
    )(got, cands, w_hidden, b_hidden.reshape(1, -1), w_out.reshape(1, -1))


def on_device(
    parts, users, behaviors, cluster_ids, lengths, candidates, w_query, w_key, w_hidden, b_hidden, w_out
):
    place = lax.axis_index("seq")
    flip = 4 * (place & 1) + (place & 2)
    scalars = jnp.stack([lengths[0, 0], flip.astype(jnp.int32)])
    bits, digits = digit_plan(parts, behaviors.shape[1])
    send, following, mine = pool(behaviors[0], cluster_ids, scalars, parts)

    def swap(value, step):
        return lax.ppermute(value, "seq", [(i, i ^ step) for i in range(parts)])

    pair = swap(send, 1).astype(F32)
    beside = swap((following + pair[1]).astype(BF), 2)
    total = mine + pair[0] + beside.astype(F32)
    own, step = total.astype(BF), SHARERS
    got = swap(own, step)
    candidates_in, got = lax.optimization_barrier((candidates, got))
    group = SHARERS * users
    groups = [[g * group + k for k in range(group)] for g in range(parts // SHARERS)]

    def exchange(value):
        return lax.all_to_all(
            value, ("seq", "cand"), 0, 0, tiled=True, axis_index_groups=groups
        )

    local, width = candidates.shape[1:]
    gathered = exchange(jnp.tile(candidates_in, (SHARERS, 1, 1)))
    while step * 2 < parts:
        step *= 2
        own = (own.astype(F32) + got.astype(F32)).astype(BF)
        got = swap(own, step)
    partial = attend(own, got, gathered.reshape(group * local, width), w_query, w_key, bits, digits)
    back = exchange(partial.reshape(group, local, 2 * width))
    return rank(back, candidates, w_hidden, b_hidden, w_out)


def solution(mesh):
    in_specs = (
        P("cand", "seq", None),
        P("cand", "seq"),
        P("cand", "seq"),
        P(None, ("seq", "cand"), None),
        P(),
        P(),
        P(),
        P(),
        P(),
    )
    out_specs = P(None, ("seq", "cand"))
    return jax.shard_map(
        functools.partial(on_device, mesh.shape["seq"], mesh.shape["cand"]),
        mesh=mesh,
        in_specs=in_specs,
        out_specs=out_specs,
        check_vma=False,
    )
```

```python
import functools

import jax
import jax.numpy as jnp
from jax import lax
from jax.experimental import pallas as pl
from jax.experimental.pallas import tpu as pltpu
from jax.sharding import PartitionSpec as P

CLUSTERS = 2048
BF = jnp.bfloat16
F32 = jnp.float32
PAD = 16
SHARERS = 4
NT = (((1,), (1,)), ((), ()))
TN = (((0,), (0,)), ((), ()))
NN = (((1,), (0,)), ((), ()))


def digit_plan(parts, slots):
    bits = 1
    while parts * (2 ** (bits + 1) - 1) <= 256:
        bits += 1
    return bits, -(-(slots.bit_length()) // bits)


def split(ids, slots_before, live, flip, first, low):
    slot = slots_before + lax.broadcasted_iota(jnp.int32, ids.shape, 1)
    high = ((ids >> (low.bit_length() - 1)) ^ flip) - first
    high = jnp.where(slot < live, high, -PAD)
    return high.astype(F32).astype(BF), (ids & (low - 1)).astype(F32).astype(BF)


def labels(count):
    return lax.broadcasted_iota(jnp.int32, (count, 1), 0).astype(F32).astype(BF)


def pooled(turned, high, within, low, groups):
    onehot = jnp.where(labels(low) == within, BF(1), BF(0))
    pieces = [jnp.where(high == BF(h), turned, BF(0)) for h in range(groups)]
    pieces.append(jnp.where(labels(PAD) == high, BF(1), BF(0)))
    return lax.dot_general(jnp.concatenate(pieces, 0), onehot, NT, preferred_element_type=F32)


def give(total, width, bits, digits, dests):
    groups = 2 * len(dests)
    counts = total[groups * width :, :].astype(jnp.int32)
    row = lax.broadcasted_iota(jnp.int32, (PAD, 1), 0)
    for pair, dest in enumerate(dests):
        tally = jnp.zeros((PAD, total.shape[1]), jnp.int32)
        for k in range(2):
            for d in range(digits):
                one = (counts[2 * pair + k : 2 * pair + k + 1, :] >> (bits * d)) & (2**bits - 1)
                tally = jnp.where(row == k * digits + d, one, tally)
        dest[: 2 * width, :] = total[2 * pair * width : 2 * (pair + 1) * width, :].astype(dest.dtype)
        dest[2 * width :, :] = tally.astype(F32).astype(dest.dtype)


def flip_of(axis):
    place = lax.axis_index(axis)
    return (place & 1) * 2 + (place & 2) * 2


def far_kernel(low, bits, digits, live, ids_ref, rows_ref, send_ref, keep_ref, turned_ref, total):
    step, steps = pl.program_id(0), pl.num_programs(0)
    block, width = rows_ref.shape
    turned = jnp.transpose(rows_ref[...].astype(BF))
    turned_ref[...] = turned
    high, within = split(ids_ref[...], step * block, live[0, 0], flip_of("seq"), SHARERS, low)
    part = pooled(turned, high, within, low, SHARERS)

    @pl.when(step == 0)
    def _():
        total[...] = part

    @pl.when(step > 0)
    def _():
        total[...] += part

    @pl.when(step == steps - 1)
    def _():
        give(total[...], width, bits, digits, (keep_ref, send_ref))


def near_kernel(low, bits, digits, block, live, ids_ref, turned_ref, send_ref, keep_ref, total):
    width, slots = turned_ref.shape
    for start in range(0, slots, block):
        there = slice(start, start + block)
        high, within = split(ids_ref[:, there], start, live[0, 0], flip_of("seq"), 0, low)
        part = pooled(turned_ref[:, there], high, within, low, SHARERS)
        if start == 0:
            total[...] = part
        else:
            total[...] += part
    give(total[...], width, bits, digits, (keep_ref, send_ref))


def sizes(slots, width, parts):
    low = CLUSTERS // (2 * SHARERS)
    return low, SHARERS * width + PAD, 2 * width + PAD, digit_plan(parts, slots)


def pool_far(rows, ids, lengths, parts):
    slots, width = rows.shape
    low, tall, height, plan = sizes(slots, width, parts)
    block = min(4096, slots)
    return pl.pallas_call(
        functools.partial(far_kernel, low, *plan),
        grid=(slots // block,),
        in_specs=[
            pl.BlockSpec(memory_space=pltpu.SMEM),
            pl.BlockSpec((1, block), lambda b: (0, b)),
            pl.BlockSpec((block, width), lambda b: (b, 0)),
        ],
        out_specs=[
            pl.BlockSpec((height, low), lambda b: (0, 0)),
            pl.BlockSpec((height, low), lambda b: (0, 0)),
            pl.BlockSpec((width, block), lambda b: (0, b)),
        ],
        out_shape=[
            jax.ShapeDtypeStruct((height, low), BF),
            jax.ShapeDtypeStruct((height, low), F32),
            jax.ShapeDtypeStruct((width, slots), BF),
        ],
        scratch_shapes=[pltpu.VMEM((tall, low), F32)],
        compiler_params=pltpu.CompilerParams(vmem_limit_bytes=44 << 20),
        name="pool_far",
    )(
        lengths,
        pltpu.with_memory_space_constraint(ids, pltpu.HBM),
        pltpu.with_memory_space_constraint(rows, pltpu.HBM),
    )


def pool_near(turned, ids, lengths, parts):
    width, slots = turned.shape
    low, tall, height, plan = sizes(slots, width, parts)
    vmem = pl.BlockSpec(memory_space=pltpu.VMEM)
    return pl.pallas_call(
        functools.partial(near_kernel, low, *plan, min(2048, slots)),
        in_specs=[pl.BlockSpec(memory_space=pltpu.SMEM), vmem, vmem],
        out_specs=[vmem, vmem],
        out_shape=[
            jax.ShapeDtypeStruct((height, low), BF),
            jax.ShapeDtypeStruct((height, low), F32),
        ],
        scratch_shapes=[pltpu.VMEM((tall, low), F32)],
        compiler_params=pltpu.CompilerParams(vmem_limit_bytes=44 << 20),
        name="pool_near",
    )(lengths, ids, turned)


def attend_kernel(width, users, bits, digits, own_ref, got_ref, cand_ref, other_ref, wq_ref, wk_ref, out_ref):
    cands = jnp.concatenate([cand_ref[...], other_ref[...]], 0)
    queries = jnp.dot(cands, wq_ref[...], preferred_element_type=F32).astype(BF)
    total = own_ref[...].astype(F32) + got_ref[...].astype(F32)
    centroids, keys, biases = [], [], []
    for k in range(2):
        count = jnp.zeros((1, total.shape[1]), F32)
        for d in range(digits):
            row = 2 * width + k * digits + d
            count = count + total[row : row + 1, :] * F32(2 ** (bits * d))
        here = (total[k * width : (k + 1) * width, :] / jnp.maximum(count, 1.0)).astype(BF)
        centroids.append(here)
        keys.append(
            lax.dot_general(wk_ref[...], here, TN, preferred_element_type=F32).astype(BF)
        )
        bias = jnp.where(count > 0, jnp.log(1.0 + count), F32(-1e9))
        biases.append(bias.astype(BF).astype(F32))
    centroids = jnp.concatenate(centroids, 1)
    keys = jnp.concatenate(keys, 1)
    biases = jnp.concatenate(biases, 1)
    scores = jnp.dot(queries, keys, preferred_element_type=F32) * F32(width**-0.5) + biases
    peak = jnp.max(scores, axis=1, keepdims=True)
    weights = jnp.exp(scores - peak)
    mass = jnp.sum(weights, axis=1, keepdims=True)
    attended = lax.dot_general(weights.astype(BF), centroids, NT, preferred_element_type=F32)
    level = peak + jnp.log(mass)
    first = level.astype(BF).astype(F32)
    second = (level - first).astype(BF).astype(F32)
    third = level - first - second
    lane = lax.broadcasted_iota(jnp.int32, attended.shape, 1)
    levels = jnp.where(lane == 0, first, jnp.where(lane == 1, second, jnp.where(lane == 2, third, 0.0)))
    result = jnp.concatenate([(attended / mass).astype(BF), levels.astype(BF)], 1)
    local = out_ref.shape[1]
    place, user = lax.axis_index("seq") & (SHARERS - 1), lax.axis_index("cand")
    for r in range(SHARERS):
        for u in range(users):
            start = (r * users + u) * local
            out_ref[(place ^ r) * users + (user ^ u)] = result[start : start + local, :]


def attend(own, got, cands, others, w_query, w_key, users, bits, digits):
    width = w_key.shape[0]
    group = SHARERS * users
    return pl.pallas_call(
        functools.partial(attend_kernel, width, users, bits, digits),
        out_shape=jax.ShapeDtypeStruct((group, 2 * cands.shape[0] // group, 2 * width), BF),
        compiler_params=pltpu.CompilerParams(vmem_limit_bytes=24 << 20),
        name="attend",
    )(own, got, cands, others, w_query, w_key)


def rank_kernel(users, got_ref, cand_ref, wh_ref, bh_ref, wo_ref, out_ref):
    width = cand_ref.shape[2]
    local = cand_ref.shape[1]
    joined = []
    for user in range(users):
        parts, levels = [], []
        for r in range(SHARERS):
            one = got_ref[r * users + user].astype(F32)
            parts.append(one[:, :width])
            levels.append(jnp.sum(one[:, width:], axis=1, keepdims=True))
        peak = functools.reduce(jnp.maximum, levels)
        shares = [jnp.exp(level - peak) for level in levels]
        mass = functools.reduce(jnp.add, shares)
        top = functools.reduce(jnp.add, [s * p for s, p in zip(shares, parts)])
        joined.append((top / mass).astype(BF))
    attended = jnp.concatenate(joined, 0)
    cands = cand_ref[...].reshape(users * local, width)
    hidden = jnp.dot(cands, wh_ref[:width, :], preferred_element_type=F32)
    hidden = hidden + jnp.dot(attended, wh_ref[width:, :], preferred_element_type=F32)
    hidden = jnp.maximum(hidden + bh_ref[...], 0.0) * wo_ref[...]
    lanes = 128
    folded = functools.reduce(
        jnp.add, [hidden[:, k : k + lanes] for k in range(0, hidden.shape[1], lanes)]
    )
    ranking = jnp.sum(jnp.transpose(folded), axis=0, keepdims=True)
    for user in range(users):
        out_ref[user : user + 1, :] = ranking[:, user * local : (user + 1) * local]


def rank(got, cands, w_hidden, b_hidden, w_out):
    users, local, width = cands.shape
    return pl.pallas_call(
        functools.partial(rank_kernel, users),
        out_shape=jax.ShapeDtypeStruct((users, local), F32),
        compiler_params=pltpu.CompilerParams(vmem_limit_bytes=16 << 20),
        name="rank",
    )(got, cands, w_hidden, b_hidden.reshape(1, -1), w_out.reshape(1, -1))


def on_device(
    parts, users, behaviors, cluster_ids, lengths, candidates, w_query, w_key, w_hidden, b_hidden, w_out
):
    bits, digits = digit_plan(parts, behaviors.shape[1])

    def swap(value, step, axis="seq", count=parts):
        return lax.ppermute(value, axis, [(i, i ^ step) for i in range(count)])

    def after(value, earlier):
        return lax.optimization_barrier((value, earlier))

    send, beyond, turned = pool_far(behaviors[0], cluster_ids, lengths, parts)
    got = swap(send, 1)
    turned, got = after(turned, got)
    beside = swap((beyond + got.astype(F32)).astype(BF), 2)
    send, mine = pool_near(turned, cluster_ids, lengths, parts)
    candidates_in, send = after(candidates, send)
    got = swap(send, 1)
    asked = jnp.stack([candidates_in, swap(candidates_in, 1)], 1)
    own = (mine + got.astype(F32) + beside.astype(F32)).astype(BF)
    asked, own = after(asked, own)
    step = SHARERS
    got = swap(own, step)
    user = lax.axis_index("cand")
    asked = [lax.dynamic_index_in_dim(asked, user ^ u, 0, False) for u in range(users)]
    asked = asked[:1] + [swap(asked[u], u, "cand", users) for u in range(1, users)]
    asked = jnp.stack(asked, 1).reshape(2 * users * candidates.shape[1], -1)
    while step * 2 < parts:
        step *= 2
        own = (own.astype(F32) + got.astype(F32)).astype(BF)
        asked, own = after(asked, own)
        got = swap(own, step)
    partial = attend(own, got, asked, swap(asked, 2), w_query, w_key, users, bits, digits)
    group = SHARERS * users
    groups = [[g * group + k for k in range(group)] for g in range(parts // SHARERS)]
    back = lax.all_to_all(partial, ("seq", "cand"), 0, 0, tiled=True, axis_index_groups=groups)
    return rank(back, candidates, w_hidden, b_hidden, w_out)


def solution(mesh):
    in_specs = (
        P("cand", "seq", None),
        P("cand", "seq"),
        P("cand", "seq"),
        P(None, ("seq", "cand"), None),
        P(),
        P(),
        P(),
        P(),
        P(),
    )
    out_specs = P(None, ("seq", "cand"))
    return jax.shard_map(
        functools.partial(on_device, mesh.shape["seq"], mesh.shape["cand"]),
        mesh=mesh,
        in_specs=in_specs,
        out_specs=out_specs,
        check_vma=False,
    )
```

```python
import functools

import jax
import jax.numpy as jnp
from jax import lax
from jax.experimental import pallas as pl
from jax.experimental.pallas import tpu as pltpu
from jax.sharding import PartitionSpec as P

CLUSTERS = 2048
BF = jnp.bfloat16
F32 = jnp.float32
PAD = 16
SHARERS = 4
NT = (((1,), (1,)), ((), ()))
TN = (((0,), (0,)), ((), ()))
NN = (((1,), (0,)), ((), ()))


def digit_plan(parts, slots):
    bits = 1
    while parts * (2 ** (bits + 1) - 1) <= 256:
        bits += 1
    return bits, -(-(slots.bit_length()) // bits)


def split(ids, slots_before, live, flip, first, low):
    slot = slots_before + lax.broadcasted_iota(jnp.int32, ids.shape, 1)
    high = ((ids >> (low.bit_length() - 1)) ^ flip) - first
    high = jnp.where(slot < live, high, -PAD)
    return high.astype(F32).astype(BF), (ids & (low - 1)).astype(F32).astype(BF)


def labels(count):
    return lax.broadcasted_iota(jnp.int32, (count, 1), 0).astype(F32).astype(BF)


def pooled(turned, high, within, low, groups):
    onehot = jnp.where(labels(low) == within, BF(1), BF(0))
    pieces = [jnp.where(high == BF(h), turned, BF(0)) for h in range(groups)]
    pieces.append(jnp.where(labels(PAD) == high, BF(1), BF(0)))
    return lax.dot_general(jnp.concatenate(pieces, 0), onehot, NT, preferred_element_type=F32)


def give(total, width, bits, digits, dests):
    groups = 2 * len(dests)
    counts = total[groups * width :, :].astype(jnp.int32)
    row = lax.broadcasted_iota(jnp.int32, (PAD, 1), 0)
    for pair, dest in enumerate(dests):
        tally = jnp.zeros((PAD, total.shape[1]), jnp.int32)
        for k in range(2):
            for d in range(digits):
                one = (counts[2 * pair + k : 2 * pair + k + 1, :] >> (bits * d)) & (2**bits - 1)
                tally = jnp.where(row == k * digits + d, one, tally)
        dest[: 2 * width, :] = total[2 * pair * width : 2 * (pair + 1) * width, :].astype(dest.dtype)
        dest[2 * width :, :] = tally.astype(F32).astype(dest.dtype)


def flip_of(axis):
    place = lax.axis_index(axis)
    return (place & 1) * 2 + (place & 2) * 2


def far_kernel(low, bits, digits, live, ids_ref, rows_ref, send_ref, keep_ref, turned_ref, total):
    step, steps = pl.program_id(0), pl.num_programs(0)
    block, width = rows_ref.shape
    turned = jnp.transpose(rows_ref[...].astype(BF))
    turned_ref[...] = turned
    high, within = split(ids_ref[...], step * block, live[0, 0], flip_of("seq"), SHARERS, low)
    part = pooled(turned, high, within, low, SHARERS)

    @pl.when(step == 0)
    def _():
        total[...] = part

    @pl.when(step > 0)
    def _():
        total[...] += part

    @pl.when(step == steps - 1)
    def _():
        give(total[...], width, bits, digits, (keep_ref, send_ref))


def near_kernel(low, bits, digits, block, live, ids_ref, turned_ref, send_ref, keep_ref, total):
    width, slots = turned_ref.shape
    for start in range(0, slots, block):
        there = slice(start, start + block)
        high, within = split(ids_ref[:, there], start, live[0, 0], flip_of("seq"), 0, low)
        part = pooled(turned_ref[:, there], high, within, low, SHARERS)
        if start == 0:
            total[...] = part
        else:
            total[...] += part
    give(total[...], width, bits, digits, (keep_ref, send_ref))


def sizes(slots, width, parts):
    low = CLUSTERS // (2 * SHARERS)
    return low, SHARERS * width + PAD, 2 * width + PAD, digit_plan(parts, slots)


def pool_far(rows, ids, lengths, parts):
    slots, width = rows.shape
    low, tall, height, plan = sizes(slots, width, parts)
    block = min(4096, slots)
    return pl.pallas_call(
        functools.partial(far_kernel, low, *plan),
        grid=(slots // block,),
        in_specs=[
            pl.BlockSpec(memory_space=pltpu.SMEM),
            pl.BlockSpec((1, block), lambda b: (0, b)),
            pl.BlockSpec((block, width), lambda b: (b, 0)),
        ],
        out_specs=[
            pl.BlockSpec((height, low), lambda b: (0, 0)),
            pl.BlockSpec((height, low), lambda b: (0, 0)),
            pl.BlockSpec((width, block), lambda b: (0, b)),
        ],
        out_shape=[
            jax.ShapeDtypeStruct((height, low), BF),
            jax.ShapeDtypeStruct((height, low), F32),
            jax.ShapeDtypeStruct((width, slots), BF),
        ],
        scratch_shapes=[pltpu.VMEM((tall, low), F32)],
        compiler_params=pltpu.CompilerParams(vmem_limit_bytes=44 << 20),
        name="pool_far",
    )(
        lengths,
        pltpu.with_memory_space_constraint(ids, pltpu.HBM),
        pltpu.with_memory_space_constraint(rows, pltpu.HBM),
    )


def pool_near(turned, ids, lengths, parts):
    width, slots = turned.shape
    low, tall, height, plan = sizes(slots, width, parts)
    vmem = pl.BlockSpec(memory_space=pltpu.VMEM)
    return pl.pallas_call(
        functools.partial(near_kernel, low, *plan, min(2048, slots)),
        in_specs=[pl.BlockSpec(memory_space=pltpu.SMEM), vmem, vmem],
        out_specs=[vmem, vmem],
        out_shape=[
            jax.ShapeDtypeStruct((height, low), BF),
            jax.ShapeDtypeStruct((height, low), F32),
        ],
        scratch_shapes=[pltpu.VMEM((tall, low), F32)],
        compiler_params=pltpu.CompilerParams(vmem_limit_bytes=44 << 20),
        cost_estimate=pl.CostEstimate(
            flops=2 * tall * low * slots, bytes_accessed=2 * width * slots, transcendentals=0
        ),
        name="pool_near",
    )(lengths, ids, turned)


def attend_kernel(width, users, bits, digits, own_ref, got_ref, cand_ref, other_ref, wq_ref, wk_ref, out_ref):
    cands = jnp.concatenate([cand_ref[...], other_ref[...]], 0)
    queries = jnp.dot(cands, wq_ref[...], preferred_element_type=F32).astype(BF)
    total = own_ref[...].astype(F32) + got_ref[...].astype(F32)
    centroids, keys, biases = [], [], []
    for k in range(2):
        count = jnp.zeros((1, total.shape[1]), F32)
        for d in range(digits):
            row = 2 * width + k * digits + d
            count = count + total[row : row + 1, :] * F32(2 ** (bits * d))
        here = (total[k * width : (k + 1) * width, :] / jnp.maximum(count, 1.0)).astype(BF)
        centroids.append(here)
        keys.append(
            lax.dot_general(wk_ref[...], here, TN, preferred_element_type=F32).astype(BF)
        )
        bias = jnp.where(count > 0, jnp.log(1.0 + count), F32(-1e9))
        biases.append(bias.astype(BF).astype(F32))
    centroids = jnp.concatenate(centroids, 1)
    keys = jnp.concatenate(keys, 1)
    biases = jnp.concatenate(biases, 1)
    scores = jnp.dot(queries, keys, preferred_element_type=F32) * F32(width**-0.5) + biases
    peak = jnp.max(scores, axis=1, keepdims=True)
    weights = jnp.exp(scores - peak)
    mass = jnp.sum(weights, axis=1, keepdims=True)
    attended = lax.dot_general(weights.astype(BF), centroids, NT, preferred_element_type=F32)
    level = peak + jnp.log(mass)
    first = level.astype(BF).astype(F32)
    second = (level - first).astype(BF).astype(F32)
    third = level - first - second
    lane = lax.broadcasted_iota(jnp.int32, attended.shape, 1)
    levels = jnp.where(lane == 0, first, jnp.where(lane == 1, second, jnp.where(lane == 2, third, 0.0)))
    result = jnp.concatenate([(attended / mass).astype(BF), levels.astype(BF)], 1)
    local = out_ref.shape[1]
    place, user = lax.axis_index("seq") & (SHARERS - 1), lax.axis_index("cand")
    for r in range(SHARERS):
        for u in range(users):
            start = (r * users + u) * local
            out_ref[(place ^ r) * users + (user ^ u)] = result[start : start + local, :]


def attend(own, got, cands, others, w_query, w_key, users, bits, digits):
    width = w_key.shape[0]
    group = SHARERS * users
    return pl.pallas_call(
        functools.partial(attend_kernel, width, users, bits, digits),
        out_shape=jax.ShapeDtypeStruct((group, 2 * cands.shape[0] // group, 2 * width), BF),
        compiler_params=pltpu.CompilerParams(vmem_limit_bytes=24 << 20),
        name="attend",
    )(own, got, cands, others, w_query, w_key)


def rank_kernel(users, got_ref, base_ref, wh_ref, wo_ref, out_ref):
    width = got_ref.shape[2] // 2
    local = got_ref.shape[1]
    joined = []
    for user in range(users):
        parts, levels = [], []
        for r in range(SHARERS):
            one = got_ref[r * users + user].astype(F32)
            parts.append(one[:, :width])
            levels.append(jnp.sum(one[:, width:], axis=1, keepdims=True))
        peak = functools.reduce(jnp.maximum, levels)
        shares = [jnp.exp(level - peak) for level in levels]
        mass = functools.reduce(jnp.add, shares)
        top = functools.reduce(jnp.add, [s * p for s, p in zip(shares, parts)])
        joined.append((top / mass).astype(BF))
    attended = jnp.concatenate(joined, 0)
    hidden = base_ref[...] + jnp.dot(attended, wh_ref[width:, :], preferred_element_type=F32)
    hidden = jnp.maximum(hidden, 0.0) * wo_ref[...]
    lanes = 128
    folded = functools.reduce(
        jnp.add, [hidden[:, k : k + lanes] for k in range(0, hidden.shape[1], lanes)]
    )
    ranking = jnp.sum(jnp.transpose(folded), axis=0, keepdims=True)
    for user in range(users):
        out_ref[user : user + 1, :] = ranking[:, user * local : (user + 1) * local]


def rank(got, base, w_hidden, w_out, users):
    return pl.pallas_call(
        functools.partial(rank_kernel, users),
        out_shape=jax.ShapeDtypeStruct((users, got.shape[1]), F32),
        compiler_params=pltpu.CompilerParams(vmem_limit_bytes=16 << 20),
        name="rank",
    )(got, base, w_hidden, w_out.reshape(1, -1))


def on_device(
    parts, users, behaviors, cluster_ids, lengths, candidates, w_query, w_key, w_hidden, b_hidden, w_out
):
    bits, digits = digit_plan(parts, behaviors.shape[1])

    def swap(value, step, axis="seq", count=parts):
        return lax.ppermute(value, axis, [(i, i ^ step) for i in range(count)])

    def after(value, earlier):
        return lax.optimization_barrier((value, earlier))

    user = lax.axis_index("cand")
    send, beyond, turned = pool_far(behaviors[0], cluster_ids, lengths, parts)
    got = swap(send, 1)
    turned, got = after(turned, got)
    beside = swap((beyond + got.astype(F32)).astype(BF), 2)
    send, mine = pool_near(turned, cluster_ids, lengths, parts)
    got = swap(send, 1)
    candidates_in, mine = after(candidates, mine + beside.astype(F32))
    asked = [lax.dynamic_index_in_dim(candidates_in, user ^ u, 0, False) for u in range(users)]
    asked = asked[:1] + [swap(asked[u], u, "cand", users) for u in range(1, users)]
    asked = jnp.concatenate(asked, 0)
    asked = jnp.concatenate([asked, swap(asked, 1)], 0)
    own = (mine + got.astype(F32)).astype(BF)
    step = SHARERS
    got = swap(own, step)
    while step * 2 < parts:
        step *= 2
        own = (own.astype(F32) + got.astype(F32)).astype(BF)
        asked, candidates_in, own = lax.optimization_barrier((asked, candidates_in, own))
        got = swap(own, step)
    width = candidates.shape[2]
    base = jnp.dot(
        candidates_in.reshape(-1, width), w_hidden[:width], preferred_element_type=F32
    )
    base = base + b_hidden
    partial = attend(own, got, asked, swap(asked, 2), w_query, w_key, users, bits, digits)
    group = SHARERS * users
    groups = [[g * group + k for k in range(group)] for g in range(parts // SHARERS)]
    back = lax.all_to_all(partial, ("seq", "cand"), 0, 0, tiled=True, axis_index_groups=groups)
    return rank(back, base, w_hidden, w_out, users)


def solution(mesh):
    in_specs = (
        P("cand", "seq", None),
        P("cand", "seq"),
        P("cand", "seq"),
        P(None, ("seq", "cand"), None),
        P(),
        P(),
        P(),
        P(),
        P(),
    )
    out_specs = P(None, ("seq", "cand"))
    return jax.shard_map(
        functools.partial(on_device, mesh.shape["seq"], mesh.shape["cand"]),
        mesh=mesh,
        in_specs=in_specs,
        out_specs=out_specs,
        check_vma=False,
    )
```

```python
import functools

import jax
import jax.numpy as jnp
from jax import lax
from jax.experimental import pallas as pl
from jax.experimental.pallas import tpu as pltpu
from jax.sharding import PartitionSpec as P

CLUSTERS = 2048
BF = jnp.bfloat16
F32 = jnp.float32
PAD = 16
SHARERS = 4
FIRST_BLOCK = 4096
NEXT_BLOCK = 2048
NT = (((1,), (1,)), ((), ()))
TN = (((0,), (0,)), ((), ()))
NN = (((1,), (0,)), ((), ()))


def digit_plan(parts, slots):
    bits = 1
    while parts * (2 ** (bits + 1) - 1) <= 256:
        bits += 1
    return bits, -(-(slots.bit_length()) // bits)


def split(marked, first, low):
    high = (marked >> (low.bit_length() - 1)) - first
    return high.astype(F32).astype(BF), (marked & (low - 1)).astype(F32).astype(BF)


def labels(count):
    return lax.broadcasted_iota(jnp.int32, (count, 1), 0).astype(F32).astype(BF)


def pooled(turned, high, within, low, groups):
    onehot = jnp.where(labels(low) == within, BF(1), BF(0))
    pieces = [jnp.where(high == BF(h), turned, BF(0)) for h in range(groups)]
    pieces.append(jnp.where(labels(PAD) == high, BF(1), BF(0)))
    return lax.dot_general(jnp.concatenate(pieces, 0), onehot, NT, preferred_element_type=F32)


def give(total, width, bits, digits, dests):
    groups = 2 * len(dests)
    counts = total[groups * width :, :].astype(jnp.int32)
    row = lax.broadcasted_iota(jnp.int32, (PAD, 1), 0)
    for pair, dest in enumerate(dests):
        tally = jnp.zeros((PAD, total.shape[1]), jnp.int32)
        for k in range(2):
            for d in range(digits):
                one = (counts[2 * pair + k : 2 * pair + k + 1, :] >> (bits * d)) & (2**bits - 1)
                tally = jnp.where(row == k * digits + d, one, tally)
        dest[: 2 * width, :] = total[2 * pair * width : 2 * (pair + 1) * width, :].astype(dest.dtype)
        dest[2 * width :, :] = tally.astype(F32).astype(dest.dtype)


def flip_of(axis):
    place = lax.axis_index(axis)
    return (place & 1) * 2 + (place & 2) * 2


def first_kernel(
    low, bits, digits, live_ref, ids_ref, rows_ref, send_ref, turned_ref, marked_ref, total
):
    step, steps = pl.program_id(0), pl.num_programs(0)
    block, width = rows_ref.shape
    turned = jnp.transpose(rows_ref[...].astype(BF))
    turned_ref[...] = turned
    slot = step * block + lax.broadcasted_iota(jnp.int32, ids_ref.shape, 1)
    marked = jnp.where(slot < live_ref[0, 0], ids_ref[...] ^ (flip_of("seq") * low), -1)
    marked_ref[...] = marked
    high, within = split(marked, 2 * SHARERS - 2, low)
    part = pooled(turned, high, within, low, 2)

    @pl.when(step == 0)
    def _():
        total[...] = part

    @pl.when(step > 0)
    def _():
        total[...] += part

    @pl.when(step == steps - 1)
    def _():
        give(total[...], width, bits, digits, (send_ref,))


def next_kernel(low, bits, digits, block, first, marked_ref, turned_ref, *refs):
    dests, total = refs[:-1], refs[-1]
    width, slots = turned_ref.shape
    for start in range(0, slots, block):
        there = slice(start, start + block)
        high, within = split(marked_ref[:, there], first, low)
        part = pooled(turned_ref[:, there], high, within, low, 2 * len(dests))
        if start == 0:
            total[...] = part
        else:
            total[...] += part
    give(total[...], width, bits, digits, dests)


def sizes(slots, width, parts):
    return CLUSTERS // (2 * SHARERS), 2 * width + PAD, digit_plan(parts, slots)


def pool_first(rows, ids, lengths, parts):
    slots, width = rows.shape
    low, height, plan = sizes(slots, width, parts)
    block = min(FIRST_BLOCK, slots)
    return pl.pallas_call(
        functools.partial(first_kernel, low, *plan),
        grid=(slots // block,),
        in_specs=[
            pl.BlockSpec(memory_space=pltpu.SMEM),
            pl.BlockSpec((1, block), lambda b: (0, b)),
            pl.BlockSpec((block, width), lambda b: (b, 0)),
        ],
        out_specs=[
            pl.BlockSpec((height, low), lambda b: (0, 0)),
            pl.BlockSpec((width, block), lambda b: (0, b)),
            pl.BlockSpec((1, block), lambda b: (0, b)),
        ],
        out_shape=[
            jax.ShapeDtypeStruct((height, low), BF),
            jax.ShapeDtypeStruct((width, slots), BF),
            jax.ShapeDtypeStruct((1, slots), jnp.int32),
        ],
        scratch_shapes=[pltpu.VMEM((height, low), F32)],
        compiler_params=pltpu.CompilerParams(vmem_limit_bytes=44 << 20),
        name="pool_first",
    )(lengths, *(pltpu.with_memory_space_constraint(v, pltpu.HBM) for v in (ids, rows)))


def pool_next(turned, marked, first, types, parts):
    width, slots = turned.shape
    low, height, plan = sizes(slots, width, parts)
    vmem = pl.BlockSpec(memory_space=pltpu.VMEM)
    tall = 2 * len(types) * width + PAD
    return pl.pallas_call(
        functools.partial(next_kernel, low, *plan, min(NEXT_BLOCK, slots), first),
        in_specs=[vmem, vmem],
        out_specs=[vmem] * len(types),
        out_shape=[jax.ShapeDtypeStruct((height, low), t) for t in types],
        scratch_shapes=[pltpu.VMEM((tall, low), F32)],
        compiler_params=pltpu.CompilerParams(vmem_limit_bytes=44 << 20),
        name="pool_next",
    )(marked, turned)


def attend_kernel(width, users, bits, digits, own_ref, got_ref, cand_ref, other_ref, wq_ref, wk_ref, out_ref):
    cands = jnp.concatenate([cand_ref[...], other_ref[...]], 0)
    queries = jnp.dot(cands, wq_ref[...], preferred_element_type=F32).astype(BF)
    total = own_ref[...].astype(F32) + got_ref[...].astype(F32)
    centroids, keys, biases = [], [], []
    for k in range(2):
        count = jnp.zeros((1, total.shape[1]), F32)
        for d in range(digits):
            row = 2 * width + k * digits + d
            count = count + total[row : row + 1, :] * F32(2 ** (bits * d))
        here = (total[k * width : (k + 1) * width, :] / jnp.maximum(count, 1.0)).astype(BF)
        centroids.append(here)
        keys.append(
            lax.dot_general(wk_ref[...], here, TN, preferred_element_type=F32).astype(BF)
        )
        bias = jnp.where(count > 0, jnp.log(1.0 + count), F32(-1e9))
        biases.append(bias.astype(BF).astype(F32))
    centroids = jnp.concatenate(centroids, 1)
    keys = jnp.concatenate(keys, 1)
    biases = jnp.concatenate(biases, 1)
    scores = jnp.dot(queries, keys, preferred_element_type=F32) * F32(width**-0.5) + biases
    peak = jnp.max(scores, axis=1, keepdims=True)
    weights = jnp.exp(scores - peak)
    mass = jnp.sum(weights, axis=1, keepdims=True)
    attended = lax.dot_general(weights.astype(BF), centroids, NT, preferred_element_type=F32)
    level = peak + jnp.log(mass)
    first = level.astype(BF).astype(F32)
    second = (level - first).astype(BF).astype(F32)
    third = level - first - second
    lane = lax.broadcasted_iota(jnp.int32, attended.shape, 1)
    levels = jnp.where(lane == 0, first, jnp.where(lane == 1, second, jnp.where(lane == 2, third, 0.0)))
    result = jnp.concatenate([(attended / mass).astype(BF), levels.astype(BF)], 1)
    local = out_ref.shape[1]
    place, user = lax.axis_index("seq") & (SHARERS - 1), lax.axis_index("cand")
    for r in range(SHARERS):
        for u in range(users):
            start = (r * users + u) * local
            out_ref[(place ^ r) * users + (user ^ u)] = result[start : start + local, :]


def attend(own, got, cands, others, w_query, w_key, users, bits, digits):
    width = w_key.shape[0]
    group = SHARERS * users
    return pl.pallas_call(
        functools.partial(attend_kernel, width, users, bits, digits),
        out_shape=jax.ShapeDtypeStruct((group, 2 * cands.shape[0] // group, 2 * width), BF),
        compiler_params=pltpu.CompilerParams(vmem_limit_bytes=24 << 20),
        name="attend",
    )(own, got, cands, others, w_query, w_key)


def rank_kernel(users, got_ref, base_ref, wh_ref, wo_ref, out_ref):
    width = got_ref.shape[2] // 2
    local = got_ref.shape[1]
    joined = []
    for user in range(users):
        parts, levels = [], []
        for r in range(SHARERS):
            one = got_ref[r * users + user].astype(F32)
            parts.append(one[:, :width])
            levels.append(jnp.sum(one[:, width:], axis=1, keepdims=True))
        peak = functools.reduce(jnp.maximum, levels)
        shares = [jnp.exp(level - peak) for level in levels]
        mass = functools.reduce(jnp.add, shares)
        top = functools.reduce(jnp.add, [s * p for s, p in zip(shares, parts)])
        joined.append((top / mass).astype(BF))
    attended = jnp.concatenate(joined, 0)
    hidden = base_ref[...] + jnp.dot(attended, wh_ref[width:, :], preferred_element_type=F32)
    hidden = jnp.maximum(hidden, 0.0) * wo_ref[...]
    lanes = 128
    folded = functools.reduce(
        jnp.add, [hidden[:, k : k + lanes] for k in range(0, hidden.shape[1], lanes)]
    )
    ranking = jnp.sum(jnp.transpose(folded), axis=0, keepdims=True)
    for user in range(users):
        out_ref[user : user + 1, :] = ranking[:, user * local : (user + 1) * local]


def rank(got, base, w_hidden, w_out, users):
    return pl.pallas_call(
        functools.partial(rank_kernel, users),
        out_shape=jax.ShapeDtypeStruct((users, got.shape[1]), F32),
        compiler_params=pltpu.CompilerParams(vmem_limit_bytes=16 << 20),
        name="rank",
    )(got, base, w_hidden, w_out.reshape(1, -1))


def on_device(
    parts, users, behaviors, cluster_ids, lengths, candidates, w_query, w_key, w_hidden, b_hidden, w_out
):
    bits, digits = digit_plan(parts, behaviors.shape[1])

    def swap(value, step, axis="seq", count=parts):
        return lax.ppermute(value, axis, [(i, i ^ step) for i in range(count)])

    def after(value, earlier):
        return lax.optimization_barrier((value, earlier))

    send, turned, marked = pool_first(behaviors[0], cluster_ids, lengths, parts)
    got = swap(send, 1)
    (beyond,) = pool_next(turned, marked, SHARERS, [F32], parts)
    turned, got = after(turned, got)
    beside = swap((beyond + got.astype(F32)).astype(BF), 2)
    mine, send = pool_next(turned, marked, 0, [F32, BF], parts)
    candidates_in, send = after(candidates, send)
    got = swap(send, 1)
    asked = jnp.stack([candidates_in, swap(candidates_in, 1)], 1)
    own = (mine + got.astype(F32) + beside.astype(F32)).astype(BF)
    asked, own = after(asked, own)
    step = SHARERS
    got = swap(own, step)
    user = lax.axis_index("cand")
    asked = [lax.dynamic_index_in_dim(asked, user ^ u, 0, False) for u in range(users)]
    asked = asked[:1] + [swap(asked[u], u, "cand", users) for u in range(1, users)]
    asked = jnp.stack(asked, 1).reshape(2 * users * candidates.shape[1], -1)
    while step * 2 < parts:
        step *= 2
        own = (own.astype(F32) + got.astype(F32)).astype(BF)
        asked, candidates_late, own = lax.optimization_barrier((asked, candidates, own))
        got = swap(own, step)
    width = candidates.shape[2]
    rows = candidates_late.reshape(-1, width)
    base = jnp.dot(rows, w_hidden[:width], preferred_element_type=F32) + b_hidden
    base, got = after(base, got)
    partial = attend(own, got, asked, swap(asked, 2), w_query, w_key, users, bits, digits)
    group = SHARERS * users
    groups = [[g * group + k for k in range(group)] for g in range(parts // SHARERS)]
    back = lax.all_to_all(partial, ("seq", "cand"), 0, 0, tiled=True, axis_index_groups=groups)
    return rank(back, base, w_hidden, w_out, users)


def solution(mesh):
    in_specs = (
        P("cand", "seq", None),
        P("cand", "seq"),
        P("cand", "seq"),
        P(None, ("seq", "cand"), None),
        P(),
        P(),
        P(),
        P(),
        P(),
    )
    out_specs = P(None, ("seq", "cand"))
    return jax.shard_map(
        functools.partial(on_device, mesh.shape["seq"], mesh.shape["cand"]),
        mesh=mesh,
        in_specs=in_specs,
        out_specs=out_specs,
        check_vma=False,
    )
```

```python
import functools

import jax
import jax.numpy as jnp
from jax import lax
from jax.experimental import pallas as pl
from jax.experimental.pallas import tpu as pltpu
from jax.sharding import PartitionSpec as P

CLUSTERS = 2048
BF = jnp.bfloat16
F32 = jnp.float32
PAD = 16
SHARERS = 4
FIRST_BLOCK = 4096
NEXT_BLOCK = 2048
NT = (((1,), (1,)), ((), ()))
TN = (((0,), (0,)), ((), ()))
NN = (((1,), (0,)), ((), ()))


def digit_plan(parts, slots):
    bits = 1
    while parts * (2 ** (bits + 1) - 1) <= 256:
        bits += 1
    return bits, -(-(slots.bit_length()) // bits)


def split(marked, first, low):
    high = (marked >> (low.bit_length() - 1)) - first
    return high.astype(F32).astype(BF), (marked & (low - 1)).astype(F32).astype(BF)


def labels(count):
    return lax.broadcasted_iota(jnp.int32, (count, 1), 0).astype(F32).astype(BF)


def pooled(turned, high, within, low, groups):
    onehot = jnp.where(labels(low) == within, BF(1), BF(0))
    pieces = [jnp.where(high == BF(h), turned, BF(0)) for h in range(groups)]
    pieces.append(jnp.where(labels(PAD) == high, BF(1), BF(0)))
    return lax.dot_general(jnp.concatenate(pieces, 0), onehot, NT, preferred_element_type=F32)


def give(total, width, bits, digits, dests):
    groups = 2 * len(dests)
    counts = total[groups * width :, :].astype(jnp.int32)
    row = lax.broadcasted_iota(jnp.int32, (PAD, 1), 0)
    for pair, dest in enumerate(dests):
        tally = jnp.zeros((PAD, total.shape[1]), jnp.int32)
        for k in range(2):
            for d in range(digits):
                one = (counts[2 * pair + k : 2 * pair + k + 1, :] >> (bits * d)) & (2**bits - 1)
                tally = jnp.where(row == k * digits + d, one, tally)
        dest[: 2 * width, :] = total[2 * pair * width : 2 * (pair + 1) * width, :].astype(dest.dtype)
        dest[2 * width :, :] = tally.astype(F32).astype(dest.dtype)


def flip_of(axis):
    place = lax.axis_index(axis)
    return (place & 1) * 2 + (place & 2) * 2


def first_kernel(
    low, bits, digits, live_ref, ids_ref, rows_ref, send_ref, turned_ref, marked_ref, total
):
    step, steps = pl.program_id(0), pl.num_programs(0)
    block, width = rows_ref.shape
    turned = jnp.transpose(rows_ref[...].astype(BF))
    there = pl.ds(pl.multiple_of(step * block, block), block)
    turned_ref[:, there] = turned
    slot = step * block + lax.broadcasted_iota(jnp.int32, ids_ref.shape, 1)
    marked = jnp.where(slot < live_ref[0, 0], ids_ref[...] ^ (flip_of("seq") * low), -1)
    marked_ref[:, there] = marked
    high, within = split(marked, 2 * SHARERS - 2, low)
    part = pooled(turned, high, within, low, 2)

    @pl.when(step == 0)
    def _():
        total[...] = part

    @pl.when(step > 0)
    def _():
        total[...] += part

    @pl.when(step == steps - 1)
    def _():
        give(total[...], width, bits, digits, (send_ref,))


def next_kernel(low, bits, digits, block, first, marked_ref, turned_ref, *refs):
    dests, total = refs[:-1], refs[-1]
    width, slots = turned_ref.shape
    for start in range(0, slots, block):
        there = slice(start, start + block)
        high, within = split(marked_ref[:, there], first, low)
        part = pooled(turned_ref[:, there], high, within, low, 2 * len(dests))
        if start == 0:
            total[...] = part
        else:
            total[...] += part
    give(total[...], width, bits, digits, dests)


def sizes(slots, width, parts):
    return CLUSTERS // (2 * SHARERS), 2 * width + PAD, digit_plan(parts, slots)


def pool_first(rows, ids, lengths, parts):
    slots, width = rows.shape
    low, height, plan = sizes(slots, width, parts)
    block = min(FIRST_BLOCK, slots)
    return pl.pallas_call(
        functools.partial(first_kernel, low, *plan),
        grid=(slots // block,),
        in_specs=[
            pl.BlockSpec(memory_space=pltpu.SMEM),
            pl.BlockSpec((1, block), lambda b: (0, b)),
            pl.BlockSpec((block, width), lambda b: (b, 0)),
        ],
        out_specs=[
            pl.BlockSpec(memory_space=pltpu.VMEM),
            pl.BlockSpec(memory_space=pltpu.VMEM),
            pl.BlockSpec(memory_space=pltpu.VMEM),
        ],
        out_shape=[
            jax.ShapeDtypeStruct((height, low), BF),
            jax.ShapeDtypeStruct((width, slots), BF),
            jax.ShapeDtypeStruct((1, slots), jnp.int32),
        ],
        scratch_shapes=[pltpu.VMEM((height, low), F32)],
        compiler_params=pltpu.CompilerParams(vmem_limit_bytes=44 << 20),
        name="pool_first",
    )(lengths, *(pltpu.with_memory_space_constraint(v, pltpu.HBM) for v in (ids, rows)))


def pool_next(turned, marked, first, types, parts):
    width, slots = turned.shape
    low, height, plan = sizes(slots, width, parts)
    vmem = pl.BlockSpec(memory_space=pltpu.VMEM)
    tall = 2 * len(types) * width + PAD
    return pl.pallas_call(
        functools.partial(next_kernel, low, *plan, min(NEXT_BLOCK, slots), first),
        in_specs=[vmem, vmem],
        out_specs=[vmem] * len(types),
        out_shape=[jax.ShapeDtypeStruct((height, low), t) for t in types],
        scratch_shapes=[pltpu.VMEM((tall, low), F32)],
        compiler_params=pltpu.CompilerParams(vmem_limit_bytes=44 << 20),
        name="pool_next",
    )(marked, turned)


def attend_kernel(width, users, bits, digits, own_ref, got_ref, cand_ref, other_ref, wq_ref, wk_ref, out_ref):
    cands = jnp.concatenate([cand_ref[...], other_ref[...]], 0)
    queries = jnp.dot(cands, wq_ref[...], preferred_element_type=F32).astype(BF)
    total = own_ref[...].astype(F32) + got_ref[...].astype(F32)
    centroids, keys, biases = [], [], []
    for k in range(2):
        count = jnp.zeros((1, total.shape[1]), F32)
        for d in range(digits):
            row = 2 * width + k * digits + d
            count = count + total[row : row + 1, :] * F32(2 ** (bits * d))
        here = (total[k * width : (k + 1) * width, :] / jnp.maximum(count, 1.0)).astype(BF)
        centroids.append(here)
        keys.append(
            lax.dot_general(wk_ref[...], here, TN, preferred_element_type=F32).astype(BF)
        )
        bias = jnp.where(count > 0, jnp.log(1.0 + count), F32(-1e9))
        biases.append(bias.astype(BF).astype(F32))
    centroids = jnp.concatenate(centroids, 1)
    keys = jnp.concatenate(keys, 1)
    biases = jnp.concatenate(biases, 1)
    scores = jnp.dot(queries, keys, preferred_element_type=F32) * F32(width**-0.5) + biases
    peak = jnp.max(scores, axis=1, keepdims=True)
    weights = jnp.exp(scores - peak)
    mass = jnp.sum(weights, axis=1, keepdims=True)
    attended = lax.dot_general(weights.astype(BF), centroids, NT, preferred_element_type=F32)
    level = peak + jnp.log(mass)
    first = level.astype(BF).astype(F32)
    second = (level - first).astype(BF).astype(F32)
    third = level - first - second
    lane = lax.broadcasted_iota(jnp.int32, attended.shape, 1)
    levels = jnp.where(lane == 0, first, jnp.where(lane == 1, second, jnp.where(lane == 2, third, 0.0)))
    result = jnp.concatenate([(attended / mass).astype(BF), levels.astype(BF)], 1)
    local = out_ref.shape[1]
    place, user = lax.axis_index("seq") & (SHARERS - 1), lax.axis_index("cand")
    for r in range(SHARERS):
        for u in range(users):
            start = (r * users + u) * local
            out_ref[(place ^ r) * users + (user ^ u)] = result[start : start + local, :]


def attend(own, got, cands, others, w_query, w_key, users, bits, digits):
    width = w_key.shape[0]
    group = SHARERS * users
    return pl.pallas_call(
        functools.partial(attend_kernel, width, users, bits, digits),
        out_shape=jax.ShapeDtypeStruct((group, 2 * cands.shape[0] // group, 2 * width), BF),
        compiler_params=pltpu.CompilerParams(vmem_limit_bytes=24 << 20),
        name="attend",
    )(own, got, cands, others, w_query, w_key)


def rank_kernel(users, got_ref, base_ref, wh_ref, wo_ref, out_ref):
    width = got_ref.shape[2] // 2
    local = got_ref.shape[1]
    joined = []
    for user in range(users):
        parts, levels = [], []
        for r in range(SHARERS):
            one = got_ref[r * users + user].astype(F32)
            parts.append(one[:, :width])
            levels.append(jnp.sum(one[:, width:], axis=1, keepdims=True))
        peak = functools.reduce(jnp.maximum, levels)
        shares = [jnp.exp(level - peak) for level in levels]
        mass = functools.reduce(jnp.add, shares)
        top = functools.reduce(jnp.add, [s * p for s, p in zip(shares, parts)])
        joined.append((top / mass).astype(BF))
    attended = jnp.concatenate(joined, 0)
    hidden = base_ref[...] + jnp.dot(attended, wh_ref[width:, :], preferred_element_type=F32)
    hidden = jnp.maximum(hidden, 0.0) * wo_ref[...]
    lanes = 128
    folded = functools.reduce(
        jnp.add, [hidden[:, k : k + lanes] for k in range(0, hidden.shape[1], lanes)]
    )
    ranking = jnp.sum(jnp.transpose(folded), axis=0, keepdims=True)
    for user in range(users):
        out_ref[user : user + 1, :] = ranking[:, user * local : (user + 1) * local]


def rank(got, base, w_hidden, w_out, users):
    return pl.pallas_call(
        functools.partial(rank_kernel, users),
        out_shape=jax.ShapeDtypeStruct((users, got.shape[1]), F32),
        compiler_params=pltpu.CompilerParams(vmem_limit_bytes=16 << 20),
        name="rank",
    )(got, base, w_hidden, w_out.reshape(1, -1))


def on_device(
    parts, users, behaviors, cluster_ids, lengths, candidates, w_query, w_key, w_hidden, b_hidden, w_out
):
    bits, digits = digit_plan(parts, behaviors.shape[1])

    def swap(value, step, axis="seq", count=parts):
        return lax.ppermute(value, axis, [(i, i ^ step) for i in range(count)])

    def after(value, earlier):
        return lax.optimization_barrier((value, earlier))

    send, turned, marked = pool_first(behaviors[0], cluster_ids, lengths, parts)
    got = swap(send, 1)
    (beyond,) = pool_next(turned, marked, SHARERS, [F32], parts)
    turned, got = after(turned, got)
    beside = swap((beyond + got.astype(F32)).astype(BF), 2)
    mine, send = pool_next(turned, marked, 0, [F32, BF], parts)
    candidates_in, send = after(candidates, send)
    got = swap(send, 1)
    asked = jnp.stack([candidates_in, swap(candidates_in, 1)], 1)
    own = (mine + got.astype(F32) + beside.astype(F32)).astype(BF)
    asked, own = after(asked, own)
    step = SHARERS
    got = swap(own, step)
    user = lax.axis_index("cand")
    asked = [lax.dynamic_index_in_dim(asked, user ^ u, 0, False) for u in range(users)]
    asked = asked[:1] + [swap(asked[u], u, "cand", users) for u in range(1, users)]
    asked = jnp.stack(asked, 1).reshape(2 * users * candidates.shape[1], -1)
    while step * 2 < parts:
        step *= 2
        own = (own.astype(F32) + got.astype(F32)).astype(BF)
        asked, candidates_late, own = lax.optimization_barrier((asked, candidates, own))
        got = swap(own, step)
    width = candidates.shape[2]
    rows = candidates_late.reshape(-1, width)
    base = jnp.dot(rows, w_hidden[:width], preferred_element_type=F32) + b_hidden
    base, got = after(base, got)
    partial = attend(own, got, asked, swap(asked, 2), w_query, w_key, users, bits, digits)
    group = SHARERS * users
    groups = [[g * group + k for k in range(group)] for g in range(parts // SHARERS)]
    back = lax.all_to_all(partial, ("seq", "cand"), 0, 0, tiled=True, axis_index_groups=groups)
    return rank(back, base, w_hidden, w_out, users)


def solution(mesh):
    in_specs = (
        P("cand", "seq", None),
        P("cand", "seq"),
        P("cand", "seq"),
        P(None, ("seq", "cand"), None),
        P(),
        P(),
        P(),
        P(),
        P(),
    )
    out_specs = P(None, ("seq", "cand"))
    return jax.shard_map(
        functools.partial(on_device, mesh.shape["seq"], mesh.shape["cand"]),
        mesh=mesh,
        in_specs=in_specs,
        out_specs=out_specs,
        check_vma=False,
    )
```

```python
import functools

import jax
import jax.numpy as jnp
from jax import lax
from jax.experimental import pallas as pl
from jax.experimental.pallas import tpu as pltpu
from jax.sharding import PartitionSpec as P

CLUSTERS = 2048
BF = jnp.bfloat16
F32 = jnp.float32
PAD = 16
SHARERS = 4
FIRST_BLOCK = 4096
NEXT_BLOCK = 2048
NT = (((1,), (1,)), ((), ()))
TN = (((0,), (0,)), ((), ()))
NN = (((1,), (0,)), ((), ()))


def digit_plan(parts, slots):
    bits = 1
    while parts * (2 ** (bits + 1) - 1) <= 256:
        bits += 1
    return bits, -(-(slots.bit_length()) // bits)


def split(marked, first, low):
    high = (marked >> (low.bit_length() - 1)) - first
    return high.astype(F32).astype(BF), (marked & (low - 1)).astype(F32).astype(BF)


def labels(count):
    return lax.broadcasted_iota(jnp.int32, (count, 1), 0).astype(F32).astype(BF)


def pooled(turned, high, within, low, groups):
    onehot = jnp.where(labels(low) == within, BF(1), BF(0))
    pieces = [jnp.where(high == BF(h), turned, BF(0)) for h in range(groups)]
    pieces.append(jnp.where(labels(PAD) == high, BF(1), BF(0)))
    return lax.dot_general(jnp.concatenate(pieces, 0), onehot, NT, preferred_element_type=F32)


def give(total, width, bits, digits, dests):
    groups = 2 * len(dests)
    counts = total[groups * width :, :].astype(jnp.int32)
    row = lax.broadcasted_iota(jnp.int32, (PAD, 1), 0)
    for pair, dest in enumerate(dests):
        tally = jnp.zeros((PAD, total.shape[1]), jnp.int32)
        for k in range(2):
            for d in range(digits):
                one = (counts[2 * pair + k : 2 * pair + k + 1, :] >> (bits * d)) & (2**bits - 1)
                tally = jnp.where(row == k * digits + d, one, tally)
        dest[: 2 * width, :] = total[2 * pair * width : 2 * (pair + 1) * width, :].astype(dest.dtype)
        dest[2 * width :, :] = tally.astype(F32).astype(dest.dtype)


def flip_of(axis):
    place = lax.axis_index(axis)
    return (place & 1) * 2 + (place & 2) * 2


def first_kernel(
    low, bits, digits, live_ref, ids_ref, rows_ref, send_ref, turned_ref, marked_ref, total
):
    step, steps = pl.program_id(0), pl.num_programs(0)
    block, width = rows_ref.shape
    turned = jnp.transpose(rows_ref[...].astype(BF))
    there = pl.ds(pl.multiple_of(step * block, block), block)
    turned_ref[:, there] = turned
    slot = step * block + lax.broadcasted_iota(jnp.int32, ids_ref.shape, 1)
    marked = jnp.where(slot < live_ref[0, 0], ids_ref[...] ^ (flip_of("seq") * low), -1)
    marked_ref[:, there] = marked
    high, within = split(marked, 2 * SHARERS - 2, low)
    part = pooled(turned, high, within, low, 2)

    @pl.when(step == 0)
    def _():
        total[...] = part

    @pl.when(step > 0)
    def _():
        total[...] += part

    @pl.when(step == steps - 1)
    def _():
        give(total[...], width, bits, digits, (send_ref,))


def next_kernel(low, bits, digits, block, first, marked_ref, turned_ref, *refs):
    dests, total = refs[:-1], refs[-1]
    width, slots = turned_ref.shape
    for start in range(0, slots, block):
        there = slice(start, start + block)
        high, within = split(marked_ref[:, there], first, low)
        part = pooled(turned_ref[:, there], high, within, low, 2 * len(dests))
        if start == 0:
            total[...] = part
        else:
            total[...] += part
    give(total[...], width, bits, digits, dests)


def sizes(slots, width, parts):
    return CLUSTERS // (2 * SHARERS), 2 * width + PAD, digit_plan(parts, slots)


def pool_first(rows, ids, lengths, parts):
    slots, width = rows.shape
    low, height, plan = sizes(slots, width, parts)
    block = min(FIRST_BLOCK, slots)
    return pl.pallas_call(
        functools.partial(first_kernel, low, *plan),
        grid=(slots // block,),
        in_specs=[
            pl.BlockSpec(memory_space=pltpu.SMEM),
            pl.BlockSpec((1, block), lambda b: (0, b)),
            pl.BlockSpec((block, width), lambda b: (b, 0)),
        ],
        out_specs=[
            pl.BlockSpec(memory_space=pltpu.VMEM),
            pl.BlockSpec(memory_space=pltpu.VMEM),
            pl.BlockSpec(memory_space=pltpu.VMEM),
        ],
        out_shape=[
            jax.ShapeDtypeStruct((height, low), BF),
            jax.ShapeDtypeStruct((width, slots), BF),
            jax.ShapeDtypeStruct((1, slots), jnp.int32),
        ],
        scratch_shapes=[pltpu.VMEM((height, low), F32)],
        compiler_params=pltpu.CompilerParams(vmem_limit_bytes=44 << 20),
        name="pool_first",
    )(lengths, *(pltpu.with_memory_space_constraint(v, pltpu.HBM) for v in (ids, rows)))


def pool_next(turned, marked, first, types, parts):
    width, slots = turned.shape
    low, height, plan = sizes(slots, width, parts)
    vmem = pl.BlockSpec(memory_space=pltpu.VMEM)
    tall = 2 * len(types) * width + PAD
    return pl.pallas_call(
        functools.partial(next_kernel, low, *plan, min(NEXT_BLOCK, slots), first),
        in_specs=[vmem, vmem],
        out_specs=[vmem] * len(types),
        out_shape=[jax.ShapeDtypeStruct((height, low), t) for t in types],
        scratch_shapes=[pltpu.VMEM((tall, low), F32)],
        compiler_params=pltpu.CompilerParams(vmem_limit_bytes=44 << 20),
        name="pool_next",
    )(marked, turned)


def attend_kernel(width, users, bits, digits, own_ref, got_ref, cand_ref, other_ref, wq_ref, wk_ref, out_ref):
    cands = jnp.concatenate([cand_ref[...], other_ref[...]], 0)
    queries = jnp.dot(cands, wq_ref[...], preferred_element_type=F32).astype(BF)
    total = own_ref[...].astype(F32) + got_ref[...].astype(F32)
    centroids, keys, biases = [], [], []
    for k in range(2):
        count = jnp.zeros((1, total.shape[1]), F32)
        for d in range(digits):
            row = 2 * width + k * digits + d
            count = count + total[row : row + 1, :] * F32(2 ** (bits * d))
        here = (total[k * width : (k + 1) * width, :] / jnp.maximum(count, 1.0)).astype(BF)
        centroids.append(here)
        keys.append(
            lax.dot_general(wk_ref[...], here, TN, preferred_element_type=F32).astype(BF)
        )
        bias = jnp.where(count > 0, jnp.log(1.0 + count), F32(-1e9))
        biases.append(bias.astype(BF).astype(F32))
    centroids = jnp.concatenate(centroids, 1)
    keys = jnp.concatenate(keys, 1)
    biases = jnp.concatenate(biases, 1)
    scores = jnp.dot(queries, keys, preferred_element_type=F32) * F32(width**-0.5) + biases
    peak = jnp.max(scores, axis=1, keepdims=True)
    weights = jnp.exp(scores - peak)
    mass = jnp.sum(weights, axis=1, keepdims=True)
    attended = lax.dot_general(weights.astype(BF), centroids, NT, preferred_element_type=F32)
    level = peak + jnp.log(mass)
    first = level.astype(BF).astype(F32)
    second = (level - first).astype(BF).astype(F32)
    third = level - first - second
    lane = lax.broadcasted_iota(jnp.int32, attended.shape, 1)
    levels = jnp.where(lane == 0, first, jnp.where(lane == 1, second, jnp.where(lane == 2, third, 0.0)))
    result = jnp.concatenate([(attended / mass).astype(BF), levels.astype(BF)], 1)
    local = out_ref.shape[1]
    place, user = lax.axis_index("seq") & (SHARERS - 1), lax.axis_index("cand")
    for r in range(SHARERS):
        for u in range(users):
            start = (r * users + u) * local
            out_ref[(place ^ r) * users + (user ^ u)] = result[start : start + local, :]


def attend(own, got, cands, others, w_query, w_key, users, bits, digits):
    width = w_key.shape[0]
    group = SHARERS * users
    return pl.pallas_call(
        functools.partial(attend_kernel, width, users, bits, digits),
        out_shape=jax.ShapeDtypeStruct((group, 2 * cands.shape[0] // group, 2 * width), BF),
        compiler_params=pltpu.CompilerParams(vmem_limit_bytes=24 << 20),
        name="attend",
    )(own, got, cands, others, w_query, w_key)


def rank_kernel(users, got_ref, base_ref, wh_ref, wo_ref, out_ref):
    width = got_ref.shape[2] // 2
    local = got_ref.shape[1]
    joined = []
    for user in range(users):
        parts, levels = [], []
        for r in range(SHARERS):
            one = got_ref[r * users + user].astype(F32)
            parts.append(one[:, :width])
            levels.append(jnp.sum(one[:, width:], axis=1, keepdims=True))
        peak = functools.reduce(jnp.maximum, levels)
        shares = [jnp.exp(level - peak) for level in levels]
        mass = functools.reduce(jnp.add, shares)
        top = functools.reduce(jnp.add, [s * p for s, p in zip(shares, parts)])
        joined.append((top / mass).astype(BF))
    attended = jnp.concatenate(joined, 0)
    hidden = base_ref[...] + jnp.dot(attended, wh_ref[width:, :], preferred_element_type=F32)
    hidden = jnp.maximum(hidden, 0.0) * wo_ref[...]
    lanes = 128
    folded = functools.reduce(
        jnp.add, [hidden[:, k : k + lanes] for k in range(0, hidden.shape[1], lanes)]
    )
    ranking = jnp.sum(jnp.transpose(folded), axis=0, keepdims=True)
    for user in range(users):
        out_ref[user : user + 1, :] = ranking[:, user * local : (user + 1) * local]


def rank(got, base, w_hidden, w_out, users):
    return pl.pallas_call(
        functools.partial(rank_kernel, users),
        out_shape=jax.ShapeDtypeStruct((users, got.shape[1]), F32),
        compiler_params=pltpu.CompilerParams(vmem_limit_bytes=16 << 20),
        name="rank",
    )(got, base, w_hidden, w_out.reshape(1, -1))


def on_device(
    parts, users, behaviors, cluster_ids, lengths, candidates, w_query, w_key, w_hidden, b_hidden, w_out
):
    bits, digits = digit_plan(parts, behaviors.shape[1])

    def swap(value, step, axis="seq", count=parts):
        return lax.ppermute(value, axis, [(i, i ^ step) for i in range(count)])

    def after(value, earlier):
        return lax.optimization_barrier((value, earlier))

    send, turned, marked = pool_first(behaviors[0], cluster_ids, lengths, parts)
    got = swap(send, 1)
    (beyond,) = pool_next(turned, marked, SHARERS, [F32], parts)
    turned, got = after(turned, got)
    beside = swap((beyond + got.astype(F32)).astype(BF), 2)
    mine, send = pool_next(turned, marked, 0, [F32, BF], parts)
    candidates_in, send = after(candidates, send)
    got = swap(send, 1)
    asked = jnp.stack([candidates_in, swap(candidates_in, 1)], 1)
    used = 2 * behaviors.shape[2] + 2 * digits
    own = (mine[:used] + got[:used].astype(F32) + beside[:used].astype(F32)).astype(BF)
    asked, own = after(asked, own)
    step = SHARERS
    got = swap(own, step)
    user = lax.axis_index("cand")
    asked = [lax.dynamic_index_in_dim(asked, user ^ u, 0, False) for u in range(users)]
    asked = asked[:1] + [swap(asked[u], u, "cand", users) for u in range(1, users)]
    asked = jnp.stack(asked, 1).reshape(2 * users * candidates.shape[1], -1)
    while step * 2 < parts:
        step *= 2
        own = (own.astype(F32) + got.astype(F32)).astype(BF)
        asked, candidates_late, own = lax.optimization_barrier((asked, candidates, own))
        got = swap(own, step)
    width = candidates.shape[2]
    rows = candidates_late.reshape(-1, width)
    base = jnp.dot(rows, w_hidden[:width], preferred_element_type=F32) + b_hidden
    base, got = after(base, got)
    partial = attend(own, got, asked, swap(asked, 2), w_query, w_key, users, bits, digits)
    group = SHARERS * users
    groups = [[g * group + k for k in range(group)] for g in range(parts // SHARERS)]
    back = lax.all_to_all(partial, ("seq", "cand"), 0, 0, tiled=True, axis_index_groups=groups)
    return rank(back, base, w_hidden, w_out, users)


def solution(mesh):
    in_specs = (
        P("cand", "seq", None),
        P("cand", "seq"),
        P("cand", "seq"),
        P(None, ("seq", "cand"), None),
        P(),
        P(),
        P(),
        P(),
        P(),
    )
    out_specs = P(None, ("seq", "cand"))
    return jax.shard_map(
        functools.partial(on_device, mesh.shape["seq"], mesh.shape["cand"]),
        mesh=mesh,
        in_specs=in_specs,
        out_specs=out_specs,
        check_vma=False,
    )
```

```python
import functools

import jax
import jax.numpy as jnp
from jax import lax
from jax.experimental import pallas as pl
from jax.experimental.pallas import tpu as pltpu
from jax.sharding import PartitionSpec as P

CLUSTERS = 2048
BF = jnp.bfloat16
F32 = jnp.float32
PAD = 16
SHARERS = 4
FIRST_BLOCK = 4096
NEXT_BLOCK = 2048
NT = (((1,), (1,)), ((), ()))
TN = (((0,), (0,)), ((), ()))
NN = (((1,), (0,)), ((), ()))


def digit_plan(parts, slots):
    bits = 1
    while parts * (2 ** (bits + 1) - 1) <= 256:
        bits += 1
    return bits, -(-(slots.bit_length()) // bits)


def split(marked, first, low):
    high = (marked >> (low.bit_length() - 1)) - first
    return high.astype(F32).astype(BF), (marked & (low - 1)).astype(F32).astype(BF)


def labels(count):
    return lax.broadcasted_iota(jnp.int32, (count, 1), 0).astype(F32).astype(BF)


def pooled(turned, high, within, low, groups):
    onehot = jnp.where(labels(low) == within, BF(1), BF(0))
    pieces = [jnp.where(high == BF(h), turned, BF(0)) for h in range(groups)]
    pieces.append(jnp.where(labels(PAD) == high, BF(1), BF(0)))
    return lax.dot_general(jnp.concatenate(pieces, 0), onehot, NT, preferred_element_type=F32)


def give(total, width, bits, digits, dests):
    groups = 2 * len(dests)
    counts = total[groups * width :, :].astype(jnp.int32)
    row = lax.broadcasted_iota(jnp.int32, (PAD, 1), 0)
    for pair, dest in enumerate(dests):
        tally = jnp.zeros((PAD, total.shape[1]), jnp.int32)
        for k in range(2):
            for d in range(digits):
                one = (counts[2 * pair + k : 2 * pair + k + 1, :] >> (bits * d)) & (2**bits - 1)
                tally = jnp.where(row == k * digits + d, one, tally)
        dest[: 2 * width, :] = total[2 * pair * width : 2 * (pair + 1) * width, :].astype(dest.dtype)
        dest[2 * width :, :] = tally.astype(F32).astype(dest.dtype)


def flip_of(axis):
    place = lax.axis_index(axis)
    return (place & 1) * 2 + (place & 2) * 2


def first_kernel(
    low, bits, digits, live_ref, ids_ref, rows_ref, send_ref, turned_ref, marked_ref, total
):
    step, steps = pl.program_id(0), pl.num_programs(0)
    block, width = rows_ref.shape
    turned = jnp.transpose(rows_ref[...].astype(BF))
    there = pl.ds(pl.multiple_of(step * block, block), block)
    turned_ref[:, there] = turned
    slot = step * block + lax.broadcasted_iota(jnp.int32, ids_ref.shape, 1)
    marked = jnp.where(slot < live_ref[0, 0], ids_ref[...] ^ (flip_of("seq") * low), -1)
    marked_ref[:, there] = marked
    high, within = split(marked, 2 * SHARERS - 2, low)
    part = pooled(turned, high, within, low, 2)

    @pl.when(step == 0)
    def _():
        total[...] = part

    @pl.when(step > 0)
    def _():
        total[...] += part

    @pl.when(step == steps - 1)
    def _():
        give(total[...], width, bits, digits, (send_ref,))


def next_kernel(low, bits, digits, block, first, marked_ref, turned_ref, *refs):
    dests, total = refs[:-1], refs[-1]
    width, slots = turned_ref.shape
    for start in range(0, slots, block):
        there = slice(start, start + block)
        high, within = split(marked_ref[:, there], first, low)
        part = pooled(turned_ref[:, there], high, within, low, 2 * len(dests))
        if start == 0:
            total[...] = part
        else:
            total[...] += part
    give(total[...], width, bits, digits, dests)


def sizes(slots, width, parts):
    return CLUSTERS // (2 * SHARERS), 2 * width + PAD, digit_plan(parts, slots)


def pool_first(rows, ids, lengths, parts):
    slots, width = rows.shape
    low, height, plan = sizes(slots, width, parts)
    block = min(FIRST_BLOCK, slots)
    return pl.pallas_call(
        functools.partial(first_kernel, low, *plan),
        grid=(slots // block,),
        in_specs=[
            pl.BlockSpec(memory_space=pltpu.SMEM),
            pl.BlockSpec((1, block), lambda b: (0, b)),
            pl.BlockSpec((block, width), lambda b: (b, 0)),
        ],
        out_specs=[
            pl.BlockSpec(memory_space=pltpu.VMEM),
            pl.BlockSpec(memory_space=pltpu.VMEM),
            pl.BlockSpec(memory_space=pltpu.VMEM),
        ],
        out_shape=[
            jax.ShapeDtypeStruct((height, low), BF),
            jax.ShapeDtypeStruct((width, slots), BF),
            jax.ShapeDtypeStruct((1, slots), jnp.int32),
        ],
        scratch_shapes=[pltpu.VMEM((height, low), F32)],
        compiler_params=pltpu.CompilerParams(vmem_limit_bytes=44 << 20),
        name="pool_first",
    )(lengths, *(pltpu.with_memory_space_constraint(v, pltpu.HBM) for v in (ids, rows)))


def pool_next(turned, marked, first, types, parts):
    width, slots = turned.shape
    low, height, plan = sizes(slots, width, parts)
    vmem = pl.BlockSpec(memory_space=pltpu.VMEM)
    tall = 2 * len(types) * width + PAD
    return pl.pallas_call(
        functools.partial(next_kernel, low, *plan, min(NEXT_BLOCK, slots), first),
        in_specs=[vmem, vmem],
        out_specs=[vmem] * len(types),
        out_shape=[jax.ShapeDtypeStruct((height, low), t) for t in types],
        scratch_shapes=[pltpu.VMEM((tall, low), F32)],
        compiler_params=pltpu.CompilerParams(vmem_limit_bytes=44 << 20),
        name="pool_next",
    )(marked, turned)


def attend_kernel(width, users, bits, digits, own_ref, got_ref, cand_ref, other_ref, wq_ref, wk_ref, out_ref):
    cands = jnp.concatenate([cand_ref[...], other_ref[...]], 0)
    queries = jnp.dot(cands, wq_ref[...], preferred_element_type=F32).astype(BF)
    total = own_ref[...].astype(F32) + got_ref[...].astype(F32)
    centroids, keys, biases = [], [], []
    for k in range(2):
        count = jnp.zeros((1, total.shape[1]), F32)
        for d in range(digits):
            row = 2 * width + k * digits + d
            count = count + total[row : row + 1, :] * F32(2 ** (bits * d))
        here = (total[k * width : (k + 1) * width, :] / jnp.maximum(count, 1.0)).astype(BF)
        centroids.append(here)
        keys.append(
            lax.dot_general(wk_ref[...], here, TN, preferred_element_type=F32).astype(BF)
        )
        bias = jnp.where(count > 0, jnp.log(1.0 + count), F32(-1e9))
        biases.append(bias.astype(BF).astype(F32))
    centroids = jnp.concatenate(centroids, 1)
    keys = jnp.concatenate(keys, 1)
    biases = jnp.concatenate(biases, 1)
    scores = jnp.dot(queries, keys, preferred_element_type=F32) * F32(width**-0.5) + biases
    peak = jnp.max(scores, axis=1, keepdims=True)
    weights = jnp.exp(scores - peak)
    mass = jnp.sum(weights, axis=1, keepdims=True)
    attended = lax.dot_general(weights.astype(BF), centroids, NT, preferred_element_type=F32)
    level = peak + jnp.log(mass)
    first = level.astype(BF).astype(F32)
    second = (level - first).astype(BF).astype(F32)
    third = level - first - second
    lane = lax.broadcasted_iota(jnp.int32, attended.shape, 1)
    levels = jnp.where(lane == 0, first, jnp.where(lane == 1, second, jnp.where(lane == 2, third, 0.0)))
    result = jnp.concatenate([(attended / mass).astype(BF), levels.astype(BF)], 1)
    local = out_ref.shape[1]
    place, user = lax.axis_index("seq") & (SHARERS - 1), lax.axis_index("cand")
    for r in range(SHARERS):
        for u in range(users):
            start = (r * users + u) * local
            out_ref[(place ^ r) * users + (user ^ u)] = result[start : start + local, :]


def attend(own, got, cands, others, w_query, w_key, users, bits, digits):
    width = w_key.shape[0]
    group = SHARERS * users
    return pl.pallas_call(
        functools.partial(attend_kernel, width, users, bits, digits),
        out_shape=jax.ShapeDtypeStruct((group, 2 * cands.shape[0] // group, 2 * width), BF),
        compiler_params=pltpu.CompilerParams(vmem_limit_bytes=24 << 20),
        name="attend",
    )(own, got, cands, others, w_query, w_key)


def rank_kernel(users, got_ref, base_ref, wh_ref, wo_ref, out_ref):
    width = got_ref.shape[2] // 2
    local = got_ref.shape[1]
    joined = []
    for user in range(users):
        parts, levels = [], []
        for r in range(SHARERS):
            one = got_ref[r * users + user].astype(F32)
            parts.append(one[:, :width])
            levels.append(jnp.sum(one[:, width:], axis=1, keepdims=True))
        peak = functools.reduce(jnp.maximum, levels)
        shares = [jnp.exp(level - peak) for level in levels]
        mass = functools.reduce(jnp.add, shares)
        top = functools.reduce(jnp.add, [s * p for s, p in zip(shares, parts)])
        joined.append((top / mass).astype(BF))
    attended = jnp.concatenate(joined, 0)
    hidden = base_ref[...] + jnp.dot(attended, wh_ref[width:, :], preferred_element_type=F32)
    hidden = jnp.maximum(hidden, 0.0) * wo_ref[...]
    lanes = 128
    folded = functools.reduce(
        jnp.add, [hidden[:, k : k + lanes] for k in range(0, hidden.shape[1], lanes)]
    )
    ranking = jnp.sum(jnp.transpose(folded), axis=0, keepdims=True)
    for user in range(users):
        out_ref[user : user + 1, :] = ranking[:, user * local : (user + 1) * local]


def rank(got, base, w_hidden, w_out, users):
    return pl.pallas_call(
        functools.partial(rank_kernel, users),
        out_shape=jax.ShapeDtypeStruct((users, got.shape[1]), F32),
        compiler_params=pltpu.CompilerParams(vmem_limit_bytes=16 << 20),
        name="rank",
    )(got, base, w_hidden, w_out.reshape(1, -1))


def on_device(
    parts, users, behaviors, cluster_ids, lengths, candidates, w_query, w_key, w_hidden, b_hidden, w_out
):
    bits, digits = digit_plan(parts, behaviors.shape[1])

    def swap(value, step, axis="seq", count=parts):
        return lax.ppermute(value, axis, [(i, i ^ step) for i in range(count)])

    def after(value, earlier):
        return lax.optimization_barrier((value, earlier))

    send, turned, marked = pool_first(behaviors[0], cluster_ids, lengths, parts)
    got = swap(send, 1)
    (beyond,) = pool_next(turned, marked, SHARERS, [F32], parts)
    turned, got = after(turned, got)
    beside = swap((beyond + got.astype(F32)).astype(BF), 2)
    mine, send = pool_next(turned, marked, 0, [F32, BF], parts)
    candidates_in, send = after(candidates, send)
    got = swap(send, 1)
    asked = jnp.stack([candidates_in, swap(candidates_in, 1)], 1)
    used = 2 * behaviors.shape[2] + 2 * digits
    own = (mine[:used] + got[:used].astype(F32) + beside[:used].astype(F32)).astype(BF)
    asked, own = after(asked, own)
    step = SHARERS
    got = swap(own, step)
    user = lax.axis_index("cand")
    asked = [lax.dynamic_index_in_dim(asked, user ^ u, 0, False) for u in range(users)]
    asked = asked[:1] + [swap(asked[u], u, "cand", users) for u in range(1, users)]
    asked = jnp.stack(asked, 1).reshape(2 * users * candidates.shape[1], -1)
    while step * 2 < parts:
        step *= 2
        own = (own.astype(F32) + got.astype(F32)).astype(BF)
        asked, candidates_late, own = lax.optimization_barrier((asked, candidates, own))
        got = swap(own, step + step // 2)
    width = candidates.shape[2]
    rows = candidates_late.reshape(-1, width)
    base = jnp.dot(rows, w_hidden[:width], preferred_element_type=F32) + b_hidden
    base, got = after(base, got)
    partial = attend(own, got, asked, swap(asked, 2), w_query, w_key, users, bits, digits)
    group = SHARERS * users
    groups = [[g * group + k for k in range(group)] for g in range(parts // SHARERS)]
    back = lax.all_to_all(partial, ("seq", "cand"), 0, 0, tiled=True, axis_index_groups=groups)
    return rank(back, base, w_hidden, w_out, users)


def solution(mesh):
    in_specs = (
        P("cand", "seq", None),
        P("cand", "seq"),
        P("cand", "seq"),
        P(None, ("seq", "cand"), None),
        P(),
        P(),
        P(),
        P(),
        P(),
    )
    out_specs = P(None, ("seq", "cand"))
    return jax.shard_map(
        functools.partial(on_device, mesh.shape["seq"], mesh.shape["cand"]),
        mesh=mesh,
        in_specs=in_specs,
        out_specs=out_specs,
        check_vma=False,
    )
```
